256 devices in a mesh: gx: 16 (over z, core), gy: 16 (over y, x).
Axes of the slice: x: 4, y: 4, z: 8, core: 2. Of those that a mesh axis runs over, the one named last changes fastest.
Arguments:
- tokens: bfloat16 [1024, 16384], P('gy', 'gx'), may hold values from -6 to 6
- gate_weight: bfloat16 [16384, 26624], P('gx', 'gy'), may hold values from -0.046875 to 0.046875
- up_weight: bfloat16 [16384, 26624], P('gx', 'gy'), may hold values from -0.046875 to 0.046875
- down_weight: bfloat16 [26624, 16384], P('gy', 'gx'), may hold values from -0.0390625 to 0.0390625
Outputs:
- mixed: float32 [1024, 16384], P('gy', 'gx')
The draws below stay inside these ranges and needn't reach their ends.
All inputs are finite; a program needn't handle non-finite values.
Results may differ from the reference program's by a relative error of at most 0.0029.
Values may be sent and summed in bfloat16 or wider, within the bound.
A program may use at most 128 MiB of HBM per device.

```python
import jax
import jax.numpy as jnp

D = 16384
FFW = 26624
TOKENS = 1024


def block_scale(key, shape, pieces, least, high):
    factor_of = 1.0
    for axis_at, shards_of in pieces:
        draws = jax.random.uniform(jax.random.fold_in(jax.random.fold_in(key, 6), axis_at), (shards_of,), jnp.float32, least / len(pieces), high / len(pieces))
        factor_of = factor_of * jnp.repeat(jnp.exp(draws), shape[axis_at] // shards_of).reshape((-1,) + (1,) * (len(shape) - 1 - axis_at))
    return factor_of


def scatter_about(rng, extent, spread, reach, split=(), dtype=jnp.bfloat16):
    factor_of = block_scale(rng, extent, split, -0.22, 0.18) if split else 1.0
    array = jax.random.normal(rng, extent, jnp.float32) * spread * factor_of
    return jnp.minimum(jnp.maximum(array, -reach), reach).astype(dtype)


def setup_inputs(seed: int = 0) -> dict:
    seeds = jax.random.split(jax.random.key(seed), 5)
    tokens = scatter_about(seeds[0], (TOKENS, D), 1.0, 6.0, ((0, 16), (1, 16)))
    gate_weight = scatter_about(seeds[1], (D, FFW), D ** -0.5, 0.046875, ((0, 16), (1, 16)))
    up_weight = scatter_about(seeds[2], (D, FFW), D ** -0.5, 0.046875, ((0, 16), (1, 16)))
    down_weight = scatter_about(seeds[3], (FFW, D), FFW ** -0.5, 0.0390625, ((0, 16), (1, 16)))
    return dict(tokens=tokens, gate_weight=gate_weight, up_weight=up_weight, down_weight=down_weight)


def reference(tokens, gate_weight, up_weight, down_weight):
    gate = jnp.dot(tokens, gate_weight, preferred_element_type=jnp.float32)
    up = jnp.dot(tokens, up_weight, preferred_element_type=jnp.float32)
    hidden = (jax.nn.silu(gate) * up).astype(jnp.bfloat16)
    return jnp.dot(hidden, down_weight, preferred_element_type=jnp.float32)
```

```python
import jax
import jax.numpy as jnp
from jax import lax
from jax.experimental import pallas as pl
from jax.experimental.pallas import tpu as pltpu
from jax.sharding import PartitionSpec as P

MESH = pl.DeviceIdType.MESH
Z = 8
ROWS = 64
HALF = 32
GATE, UP = 0, 1
LANES = 128
POWER = 7
SHIFT = 5.0


def encode(x):
    y = x * 32.0
    y2 = y * y
    y3 = y2 * y
    return (y2 * y2 * y3).astype(jnp.bfloat16)


def decode(v):
    y = v.astype(jnp.float32)
    root = jnp.exp2(jnp.log(jnp.abs(y)) * (1.4426950408889634 / POWER) - SHIFT)
    return jnp.where(y < 0.0, -root, root)


def kernel(
    tok_hbm, gate_hbm, up_hbm, down_hbm, out_ref,
    w, wd, tok, part, sib, zsend, zrecv, hid, msend, mrecv,
    lsem, tok_s, tok_r, ex_s, ex_r, rs_s, rs_r, ag_s, ag_r, sb_s, sb_r, mx_s, mx_r,
):
    gx, gy = lax.axis_index("gx"), lax.axis_index("gy")
    m, c = gx // 2, gx % 2
    gyy, gyx = gy // 4, gy % 4
    width = w.shape[2]
    tiles = width // LANES

    def at_xy(dy, dx):
        return {"gx": gx, "gy": ((gyy + dy + 8) % 4) * 4 + (gyx + dx + 8) % 4}

    def at_z(step):
        return {"gx": ((m + step + Z) % Z) * 2 + c, "gy": gy}

    other = {"gx": m * 2 + 1 - c, "gy": gy}

    def block(k):
        return (m + k + Z) % Z

    def shift_of(d, h):
        return d // 4 + 2 * h, d % 4 + 2 * h

    loads = [
        pltpu.make_async_copy(gate_hbm, w.at[GATE], lsem.at[0]),
        pltpu.make_async_copy(up_hbm, w.at[UP], lsem.at[1]),
        pltpu.make_async_copy(down_hbm, wd, lsem.at[2]),
        pltpu.make_async_copy(tok_hbm, tok.at[0], lsem.at[3]),
    ]
    for load in loads[:2] + loads[3:]:
        load.start()

    barrier = pltpu.get_barrier_semaphore()
    for there in (at_z(1), at_z(-1), other):
        pl.semaphore_signal(barrier, inc=1, device_id=there, device_id_type=MESH)
    for dy in range(4):
        for dx in range(4):
            if dy or dx:
                pl.semaphore_signal(barrier, inc=1, device_id=at_xy(dy, dx), device_id_type=MESH)
    pl.semaphore_wait(barrier, 18)

    order = [4, 3, -3, 2, -2, 1, -1, 0]

    def tok_copy(k, h):
        d = block(k)
        j = d * 2 + h
        dy, dx = shift_of(d, h)
        return j, pltpu.make_async_remote_copy(
            src_ref=tok_hbm, dst_ref=tok.at[j], send_sem=tok_s.at[j], recv_sem=tok_r.at[j],
            device_id=at_xy(-dy, -dx), device_id_type=MESH,
        )

    def tok_send(k):
        for h in range(2):
            j, copy = tok_copy(k, h)

            @pl.when(j != 0)
            def _():
                copy.start()

    def tok_wait(k):
        for h in range(2):
            j, copy = tok_copy(k, h)

            @pl.when(j != 0)
            def _():
                copy.wait_recv()

    def exchange(b, gu):
        return pltpu.make_async_remote_copy(
            src_ref=part.at[b, gu, :, pl.ds((1 - c) * HALF, HALF), :], dst_ref=sib.at[b, gu],
            send_sem=ex_s.at[b * 2 + gu], recv_sem=ex_r.at[b * 2 + gu], device_id=other, device_id_type=MESH,
        )

    def product(b, gu):
        d = block(order[b])
        wide = 2 * LANES

        def tile(start, size):
            rows = jnp.concatenate([tok[d * 2], tok[d * 2 + 1]], axis=0)
            res = jnp.dot(rows, w[gu, :, pl.ds(start, size)], preferred_element_type=jnp.float32)
            part[b, gu, 0, :, pl.ds(start, size)] = res[:ROWS]
            part[b, gu, 1, :, pl.ds(start, size)] = res[ROWS:]

        def body(i, _):
            tile(pl.multiple_of(i * wide, wide), wide)
            return 0

        lax.fori_loop(0, width // wide, body, 0)
        if width % wide:
            tile(width - width % wide, width % wide)
        exchange(b, gu).start()

    def unit_index(k, q, h):
        return h if k == 4 else 2 + (3 - k) * 4 + h * 2 + q

    def rs_copy(way, k, q, h):
        u = unit_index(k, q, h)
        return pltpu.make_async_remote_copy(
            src_ref=zsend.at[way, u], dst_ref=zrecv.at[way, u],
            send_sem=rs_s.at[way * 14 + u], recv_sem=rs_r.at[way * 14 + u],
            device_id=at_z(1 - 2 * way), device_id_type=MESH,
        )

    def matrix_of(way, q):
        return (UP, GATE)[q] if way == 0 else (GATE, UP)[q]

    def own_sum(b, gu, h, cols):
        return part[b, gu, h, pl.ds(c * HALF, HALF), cols] + sib[b, gu, h, :, cols]

    def combine(b, way, k, q, h):
        gu = matrix_of(way, q)
        arrived = (k + 1 < 4) or (k + 1 == 4 and q == 1)
        if arrived:
            rs_copy(way, k + 1, q, h).wait_recv()
            src = unit_index(k + 1, q, h)
        u = unit_index(k, q, h)
        for i in range(tiles):
            cols = pl.ds(i * LANES, LANES)
            total = own_sum(b, gu, h, cols)
            if arrived:
                total = total + decode(zrecv[way, src, :, cols])
            zsend[way, u, :, cols] = encode(total)
        rs_copy(way, k, q, h).start()

    def ag_copy(way, s, h):
        u = 6 if s == 4 else (s - 1) * 2 + h
        d = block(-(s - 1) if way == 0 else s - 1)
        place = hid.at[d, h, pl.ds(c * HALF, HALF), :]
        return pltpu.make_async_remote_copy(
            src_ref=place, dst_ref=place, send_sem=ag_s.at[way * 7 + u], recv_sem=ag_r.at[way * 7 + u],
            device_id=at_z(1 - 2 * way), device_id_type=MESH,
        )

    def ag_arrival(way, s, h):
        u = 6 if s == 4 else (s - 1) * 2 + h
        d = block(-s if way == 0 else s)
        place = hid.at[d, h, pl.ds(c * HALF, HALF), :]
        return pltpu.make_async_remote_copy(
            src_ref=place, dst_ref=place, send_sem=ag_s.at[way * 7 + u], recv_sem=ag_r.at[way * 7 + u],
            device_id=at_z(1 - 2 * way), device_id_type=MESH,
        )

    def sib_index(k, h):
        return order.index(k) * 2 + h

    def sib_copy(k, h, core):
        place = hid.at[block(k), h, pl.ds(core * HALF, HALF), :]
        i = sib_index(k, h)
        return pltpu.make_async_remote_copy(
            src_ref=place, dst_ref=place, send_sem=sb_s.at[i], recv_sem=sb_r.at[i],
            device_id=other, device_id_type=MESH,
        )

    def finish(h):
        for way in range(2):
            for q in range(2):
                rs_copy(way, 1, q, h).wait_recv()
        for i in range(tiles):
            cols = pl.ds(i * LANES, LANES)
            sums = []
            for gu in (GATE, UP):
                total = own_sum(7, gu, h, cols)
                for way in range(2):
                    q = 0 if matrix_of(way, 0) == gu else 1
                    total = total + decode(zrecv[way, unit_index(1, q, h), :, cols])
                sums.append(total)
            gate, up = sums
            hid[m, h, pl.ds(c * HALF, HALF), cols] = (gate / (1.0 + jnp.exp(-gate)) * up).astype(jnp.bfloat16)
        ag_copy(0, 1, h).start()
        ag_copy(1, 1, h).start()
        sib_copy(0, h, c).start()

    def mx_copy(k, h):
        d = block(k)
        j = d * 2 + h
        dy, dx = shift_of(d, h)
        return j, pltpu.make_async_remote_copy(
            src_ref=msend.at[j], dst_ref=mrecv.at[j], send_sem=mx_s.at[j], recv_sem=mx_r.at[j],
            device_id=at_xy(dy, dx), device_id_type=MESH,
        )

    def down(units):
        for k, h in units:
            sib_copy(k, h, 1 - c).wait_recv()
        wide = 2 * LANES

        def body(i, _):
            cols = pl.ds(pl.multiple_of(i * wide, wide), wide)
            rows = [hid[block(k), h] for k, h in units]
            rows = rows[0] if len(rows) == 1 else jnp.concatenate(rows, axis=0)
            res = jnp.dot(rows, wd[:, cols], preferred_element_type=jnp.float32).astype(jnp.bfloat16)
            for n, (k, h) in enumerate(units):
                msend[block(k) * 2 + h, :, cols] = res[n * ROWS : (n + 1) * ROWS]
            return 0

        lax.fori_loop(0, wd.shape[1] // wide, body, 0)
        for k, h in units:
            j, copy = mx_copy(k, h)

            @pl.when(j != 0)
            def _():
                copy.start()

            @pl.when(j == 0)
            def _():
                mrecv[0] = msend[0]

    tok_send(4)
    tok_send(3)
    tok_send(-3)
    loads[3].wait()
    tok_wait(4)
    for k in (2, -2, 1, -1, 0):
        tok_send(k)
    loads[0].wait()
    product(0, GATE)
    loads[1].wait()
    product(0, UP)
    loads[2].start()
    for gu, way in ((GATE, 0), (UP, 1)):
        exchange(0, gu).wait_recv()
        for h in range(2):
            combine(0, way, 4, 1, h)
    for k in (3, 2, 1):
        bs = (order.index(k), order.index(-k))
        tok_wait(k)
        tok_wait(-k)
        for q in range(2):
            for way in range(2):
                product(bs[way], matrix_of(way, q))
        for h in range(2):
            for q in range(2):
                for way in range(2):
                    if h == 0:
                        exchange(bs[way], matrix_of(way, q)).wait_recv()
                    combine(bs[way], way, k, q, h)
    tok_wait(0)
    for gu in range(2):
        product(7, gu)
    for gu in range(2):
        exchange(7, gu).wait_recv()
    finish(0)
    finish(1)
    loads[2].wait()
    waiting = [[(0, 0)], [(0, 1)]]
    for s in (1, 2, 3):
        for h in range(2):
            for way in range(2):
                ag_arrival(way, s, h).wait_recv()
                if s < 3 or way == h:
                    ag_copy(way, 4 if s == 3 else s + 1, h).start()
                sib_copy(-s if way == 0 else s, h, c).start()
            down(waiting.pop(0))
            waiting.append([(-s, h), (s, h)])
    for way in range(2):
        ag_arrival(way, 4, way).wait_recv()
        sib_copy(4, way, c).start()
    down(waiting.pop(0))
    down(waiting.pop(0))
    down([(4, 0), (4, 1)])

    for k in (0, -1, 1, -2, 2, -3, 3, 4):
        for h in range(2):
            j, copy = mx_copy(k, h)

            @pl.when(j != 0)
            def _():
                copy.wait_recv()

    def total_body(i, _):
        cols = pl.ds(pl.multiple_of(i * LANES, LANES), LANES)
        total = mrecv[0, :, cols].astype(jnp.float32)
        for j in range(1, 16):
            total = total + mrecv[j, :, cols].astype(jnp.float32)
        out_ref[:, cols] = total
        return 0

    lax.fori_loop(0, out_ref.shape[1] // LANES, total_body, 0)

    for k in order:
        for h in range(2):
            j, tcopy = tok_copy(k, h)
            _, mcopy = mx_copy(k, h)

            @pl.when(j != 0)
            def _():
                tcopy.wait_send()
                mcopy.wait_send()

            sib_copy(k, h, c).wait_send()
    for b in range(8):
        for gu in range(2):
            exchange(b, gu).wait_send()
    for way in range(2):
        for h in range(2):
            rs_copy(way, 4, 1, h).wait_send()
        for k in (3, 2, 1):
            for q in range(2):
                for h in range(2):
                    rs_copy(way, k, q, h).wait_send()
        for s in (1, 2, 3):
            for h in range(2):
                ag_copy(way, s, h).wait_send()
        ag_copy(way, 4, way).wait_send()


def local(tokens, gate_weight, up_weight, down_weight):
    rows, depth = tokens.shape
    width, columns = down_weight.shape
    anywhere = pl.BlockSpec(memory_space=pl.ANY)
    dma = pltpu.SemaphoreType.DMA
    bf16, f32 = jnp.bfloat16, jnp.float32
    return pl.pallas_call(
        kernel,
        name="gated_block",
        out_shape=jax.ShapeDtypeStruct((rows, columns), f32),
        in_specs=[anywhere] * 4,
        out_specs=pl.BlockSpec(memory_space=pltpu.VMEM),
        scratch_shapes=[
            pltpu.VMEM((2, depth, width), bf16),
            pltpu.VMEM((width, columns), bf16),
            pltpu.VMEM((16, rows, depth), bf16),
            pltpu.VMEM((8, 2, 2, rows, width), f32),
            pltpu.VMEM((8, 2, 2, HALF, width), f32),
            pltpu.VMEM((2, 14, HALF, width), bf16),
            pltpu.VMEM((2, 14, HALF, width), bf16),
            pltpu.VMEM((8, 2, rows, width), bf16),
            pltpu.VMEM((16, rows, columns), bf16),
            pltpu.VMEM((16, rows, columns), bf16),
            dma((4,)), dma((16,)), dma((16,)), dma((16,)), dma((16,)), dma((28,)), dma((28,)),
            dma((14,)), dma((14,)), dma((16,)), dma((16,)), dma((16,)), dma((16,)),
        ],
        compiler_params=pltpu.CompilerParams(
            collective_id=0, has_side_effects=True, vmem_limit_bytes=58 * 1024 * 1024
        ),
        cost_estimate=pl.CostEstimate(
            flops=2 * 16 * rows * depth * 3 * width, bytes_accessed=3 * 2 * depth * width, transcendentals=0
        ),
    )(tokens, gate_weight, up_weight, down_weight)


def solution(mesh):
    placed = (P("gy", "gx"), P("gx", "gy"), P("gx", "gy"), P("gy", "gx"))
    return jax.shard_map(
        local, mesh=mesh, in_specs=placed, out_specs=P("gy", "gx"), check_vma=False
    )
```
